32 devices in a mesh: group: 2 (over x), inner: 16 (over z, y, core).
Axes of the slice: x: 2, y: 2, z: 4, core: 2. Of those that a mesh axis runs over, the one named last changes fastest.
Arguments:
- qkv_rows: bfloat16 [4096, 2304], P(('group', 'inner')), parts along dimension 0, may hold values from -8 to 8
- pair_counts: int32 [32, 16], P('group'), parts along dimension 0, may hold values from 0 to 16, as said below
- image_dims: int32 [2, 32], P(None, 'group'), parts along dimension 1, may hold values from 0 to 4, as said below
- block_mask: int32 [32, 7], P(('group', 'inner')), parts along dimension 0, may hold values from 0 to 1, as said below
- out_weight: bfloat16 [768, 1536], replicated, may hold values from -0.21875 to 0.21875
Outputs:
- layer_out: bfloat16 [4096, 1536], P(('group', 'inner')), parts along dimension 0
The draws below stay inside these ranges and needn't reach their ends.
There are 2 independent parts, one for each index of `group`. The reference program is written for one: setup_inputs(seed, part) draws one part's arguments, and reference() takes and returns one part's arrays. A program takes and returns all parts, laid end to end along the dimension named above; an argument that names none is the same for every part. Nothing has to cross between parts.
Inputs may be any that keep to these rules, and one draw needn't show every extreme that they name: `pair_counts`: every row and every column sums to 128, and every row and every column holds an entry equal to 16. `image_dims`: widths are 1, 2 or 4; each image covers at most 4 tiles and some image is 4 tiles high and 1 wide; the tiles of all images sum to 16; images of height 0 stand only after all others. `block_mask`: column 4 - 1 (a tile with itself) is always 1.
All inputs are finite; a program needn't handle non-finite values.
Results may differ from the reference program's by a relative error of at most 0.0093.
Values may be sent and summed in bfloat16 or wider, within the bound.
A program may use at most 64 MiB of HBM per device.

```python
import math
import jax
import jax.numpy as jnp
from jax import lax

D = 1536
H = 6
HD = 128
TR = 8
TC = 16
TOK_DEV = 128
TOKENS = 2048
NB = 16
MAXT = 4
WIN = 7
CAP = 16
N_INNER = 16


def draw_qkv_rows(key, part):
    width = 3 * H * HD
    base_key = jax.random.fold_in(key, 101)
    values = jnp.clip(jax.random.normal(base_key, (TOKENS, width), jnp.float32), -6.0, 6.0)
    return values.astype(jnp.bfloat16)


def draw_pair_counts(key, part):
    half = CAP // 2
    delta = jax.random.randint(jax.random.fold_in(key, 31), (N_INNER // 2,), -half, half + 1)
    peak = jax.random.randint(jax.random.fold_in(key, 34), (), 0, N_INNER // 2)
    delta = jnp.where(jnp.arange(N_INNER // 2, dtype=jnp.int32) == peak, half, delta)
    amounts = jnp.stack([half + delta, half - delta], axis=1).reshape(N_INNER)
    send_perm = jax.random.permutation(jax.random.fold_in(key, 32), N_INNER)
    recv_perm = jax.random.permutation(jax.random.fold_in(key, 33), N_INNER)
    index_table = (recv_perm[None, :] - send_perm[:, None]) % N_INNER
    return jnp.take(amounts, index_table).astype(jnp.int32)


def draw_image_dims(key, part):
    codes = jax.random.randint(jax.random.fold_in(key, 21), (NB,), 0, 3)
    raw_high = jax.random.randint(jax.random.fold_in(key, 22), (NB,), 1, MAXT + 1)
    tall_index = jax.random.randint(jax.random.fold_in(key, 23), (), 0, 4)

    def place(remaining, inputs):
        index_now, code_now, high_now = inputs
        wide = jnp.left_shift(jnp.int32(1), code_now)
        forced = index_now == tall_index
        wide = jnp.where(forced, 1, wide)
        wide = jnp.where(wide > remaining, jnp.where(remaining >= 2, 2, 1), wide)
        high = 1 + (high_now - 1) % jnp.maximum(MAXT // wide, 1)
        high = jnp.where(forced, MAXT, high)
        high = jnp.minimum(high, remaining // wide)
        return (remaining - high * wide, jnp.stack([high, wide]))
    leftover, dims = lax.scan(place, jnp.int32(NB), (jnp.arange(NB, dtype=jnp.int32), codes, raw_high))
    return dims.T.astype(jnp.int32)


def draw_block_mask(key, part):
    mask_bits = jax.random.randint(jax.random.fold_in(key, 41), (NB, WIN), 0, 2)
    own_tile = jnp.arange(WIN, dtype=jnp.int32)[None, :] == MAXT - 1
    return jnp.where(own_tile, 1, mask_bits).astype(jnp.int32)


def gaussian(stream_key, extent, deviation, reach, kind=jnp.bfloat16):
    values = deviation * jax.random.normal(stream_key, extent, jnp.float32)
    return jnp.clip(values, min=-reach, max=reach).astype(kind)


def setup_inputs(seed: int = 0, part: int = 0) -> dict:
    seeds = jax.random.split(jax.random.key(seed), 6)
    part_splits = jax.random.split(jax.random.fold_in(seeds[5], part), 6)
    return {
        "qkv_rows": draw_qkv_rows(jax.random.fold_in(jax.random.fold_in(seeds[5], part), 71), part),
        "pair_counts": draw_pair_counts(jax.random.fold_in(jax.random.fold_in(seeds[5], part), 71), part),
        "image_dims": draw_image_dims(jax.random.fold_in(jax.random.fold_in(seeds[5], part), 71), part),
        "block_mask": draw_block_mask(jax.random.fold_in(jax.random.fold_in(seeds[5], part), 71), part),
        "out_weight": gaussian(seeds[4], (H * HD, D), (H * HD) ** -0.5, 0.21875),
    }


def block_places(blocks, image_dims):
    heights = image_dims[0]
    widths = image_dims[1]
    tile_count = heights * widths
    starts = jnp.cumsum(tile_count) - tile_count
    inside = (starts[None, :] <= blocks[:, None]).astype(jnp.int32)
    image_id = lax.optimization_barrier(jnp.sum(inside, axis=1)) - 1
    picked = jnp.arange(starts.shape[0], dtype=jnp.int32)[None, :] == image_id[:, None]
    first_block = lax.optimization_barrier(jnp.sum(jnp.where(picked, starts[None, :], 0), axis=1))
    across = jnp.maximum(lax.optimization_barrier(jnp.sum(jnp.where(picked, widths[None, :], 0), axis=1)), 1)
    local_tile = blocks - first_block
    return (image_id, local_tile // across, local_tile % across)

def rotate(rows_in, row_pos, col_pos):
    count = rows_in.shape[0]
    quarter = HD // 4
    frequency = 10000.0 ** (-jnp.arange(quarter, dtype=jnp.float32) / quarter)
    angles = jnp.stack([row_pos.astype(jnp.float32)[:, None] * frequency[None, :], col_pos.astype(jnp.float32)[:, None] * frequency[None, :]], axis=1)
    cosine = jnp.cos(angles)[:, None, :, :]
    sine_part = jnp.sin(angles)[:, None, :, :]
    split_rows = rows_in.astype(jnp.float32).reshape(count, H, 2, 2, quarter)
    leading = split_rows[:, :, :, 0, :]
    trailing = split_rows[:, :, :, 1, :]
    turned = jnp.stack([leading * cosine - trailing * sine_part, trailing * cosine + leading * sine_part], axis=3)
    return turned.reshape(count, H * HD).astype(jnp.bfloat16)

def packing_rows(pair_counts):
    column_end = jnp.cumsum(pair_counts, axis=0)
    column_start = column_end - pair_counts
    row_start = jnp.cumsum(pair_counts, axis=1) - pair_counts
    owner = jnp.arange(TOKENS, dtype=jnp.int32) // TOK_DEV
    local_row = jnp.arange(TOKENS, dtype=jnp.int32) % TOK_DEV
    ends_for = jnp.take(column_end.T, owner, axis=0)
    source = lax.optimization_barrier(jnp.sum((ends_for <= local_row[:, None]).astype(jnp.int32), axis=1))
    begin = column_start[source, owner]
    offset_row = row_start[source, owner]
    return (source * TOK_DEV + offset_row + local_row - begin).astype(jnp.int32)

def reference(qkv_rows, pair_counts, image_dims, block_mask, out_weight):
    block_rows = TR * TC
    inner_width = H * HD
    loader_row = packing_rows(pair_counts)
    packed = jnp.take(qkv_rows, loader_row, axis=0)
    all_blocks = jnp.arange(NB, dtype=jnp.int32)
    image_id, tile_row, tile_col = block_places(all_blocks, image_dims)
    within = jnp.arange(block_rows, dtype=jnp.int32)
    row_pos = (tile_row[:, None] * TR + within[None, :] // TC).reshape(-1)
    col_pos = (tile_col[:, None] * TC + within[None, :] % TC).reshape(-1)
    queries = rotate(packed[:, :inner_width], row_pos, col_pos)
    keys = rotate(packed[:, inner_width:2 * inner_width], row_pos, col_pos)
    values = packed[:, 2 * inner_width:]
    margin = (MAXT - 1) * block_rows
    keys_pad = jnp.pad(keys, ((margin, margin), (0, 0)))
    values_pad = jnp.pad(values, ((margin, margin), (0, 0)))
    score_scale = 1.0 / math.sqrt(HD)

    def one_block(block_id):
        query_blk = lax.dynamic_slice_in_dim(queries, block_id * block_rows, block_rows, 0).astype(jnp.float32).reshape(block_rows, H, HD)
        key_blk = lax.dynamic_slice_in_dim(keys_pad, block_id * block_rows, WIN * block_rows, 0).astype(jnp.float32).reshape(WIN * block_rows, H, HD)
        value_blk = lax.dynamic_slice_in_dim(values_pad, block_id * block_rows, WIN * block_rows, 0).astype(jnp.float32).reshape(WIN * block_rows, H, HD)
        key_blocks = block_id - (MAXT - 1) + jnp.arange(WIN, dtype=jnp.int32)
        in_range = (key_blocks >= 0) & (key_blocks < NB)
        same_image = jnp.take(image_id, jnp.clip(key_blocks, 0, NB - 1)) == image_id[block_id]
        mask_bits = lax.dynamic_index_in_dim(block_mask, block_id, 0, keepdims=False) == 1
        allowed = in_range & same_image & mask_bits
        visible = jnp.repeat(allowed, block_rows)[None, None, :]
        scores = jnp.einsum('qhd,khd->qhk', query_blk, key_blk) * score_scale
        scores = jnp.where(visible, scores, -1e+30)
        row_max = lax.optimization_barrier(jnp.max(scores, axis=2))
        weights = jnp.where(visible, jnp.exp(scores - row_max[:, :, None]), 0.0)
        row_sum = lax.optimization_barrier(jnp.sum(weights, axis=2))
        rounded = lax.optimization_barrier(weights.astype(jnp.bfloat16))
        mixed = jnp.einsum('qhk,khd->qhd', rounded.astype(jnp.float32), value_blk)
        return (mixed / row_sum[:, :, None]).reshape(block_rows, inner_width).astype(jnp.bfloat16)
    attended = lax.map(one_block, all_blocks).reshape(TOKENS, inner_width)
    projected = jnp.dot(attended, out_weight, preferred_element_type=jnp.float32).astype(jnp.bfloat16)
    return jnp.zeros_like(projected).at[loader_row].set(projected)
```

```python
import functools
import math

import jax
import jax.numpy as jnp
import numpy as np
from jax import lax
from jax.experimental import pallas as pl
from jax.experimental.pallas import tpu as pltpu
from jax.sharding import PartitionSpec as P

H = 6
HD = 128
TR = 8
TC = 16
SPAN = 4
MAXT = 4
WIN = 7


def running(counts):
    ids = jnp.arange(counts.shape[0], dtype=jnp.int32)
    return jnp.sum(jnp.where(ids[:, None] <= ids[None, :], counts[:, None], 0), axis=0)


def from_behind(value, axis, steps):
    count = lax.axis_size(axis)
    pairs = [(source, (source + steps) % count) for source in range(count)]
    return lax.ppermute(value, axis, pairs)


def block_places(blocks, image_dims):
    heights = image_dims[0]
    widths = image_dims[1]
    tile_count = heights * widths
    starts = running(tile_count) - tile_count
    inside = (starts[None, :] <= blocks[:, None]).astype(jnp.int32)
    image_id = jnp.sum(inside, axis=1) - 1
    picked = jnp.arange(starts.shape[0], dtype=jnp.int32)[None, :] == image_id[:, None]
    first_block = jnp.sum(jnp.where(picked, starts[None, :], 0), axis=1)
    across = jnp.maximum(jnp.sum(jnp.where(picked, widths[None, :], 0), axis=1), 1)
    local_tile = blocks - first_block
    return (image_id, local_tile // across, local_tile % across)


def rotate(rows_in, row_pos, col_pos):
    count = rows_in.shape[0]
    quarter = HD // 4
    frequency = 10000.0 ** (-jnp.arange(quarter, dtype=jnp.float32) / quarter)
    angles = jnp.stack(
        [
            row_pos.astype(jnp.float32)[:, None] * frequency[None, :],
            col_pos.astype(jnp.float32)[:, None] * frequency[None, :],
        ],
        axis=1,
    )
    cosine = jnp.cos(angles)[:, None, :, :]
    sine_part = jnp.sin(angles)[:, None, :, :]
    split_rows = rows_in.astype(jnp.float32).reshape(count, H, 2, 2, quarter)
    leading = split_rows[:, :, :, 0, :]
    trailing = split_rows[:, :, :, 1, :]
    turned = jnp.stack(
        [leading * cosine - trailing * sine_part, trailing * cosine + leading * sine_part], axis=3
    )
    return turned.reshape(count, H * HD).astype(jnp.bfloat16)


def shards(qkv_rows, pair_counts, image_dims, block_mask, out_weight):
    devices = lax.axis_size("inner")
    self_index = lax.axis_index("inner")
    tok_rows = qkv_rows.shape[0]
    full_width = qkv_rows.shape[1]
    inner_width = full_width // 3
    slot_count = 2 * tok_rows // devices
    block_rows = TR * TC
    per_device = tok_rows // block_rows
    reach_count = (SPAN * tok_rows - block_rows + tok_rows - 1) // tok_rows
    score_scale = 1.0 / math.sqrt(HD)
    sent_counts = lax.dynamic_index_in_dim(pair_counts, self_index, 0, keepdims=False)
    taken_counts = lax.dynamic_index_in_dim(pair_counts, self_index, 1, keepdims=False)
    sent_end = running(sent_counts)
    sent_start = sent_end - sent_counts
    taken_end = running(taken_counts)
    taken_start = taken_end - taken_counts
    slot_ids = jnp.arange(slot_count, dtype=jnp.int32)
    row_ids = jnp.arange(tok_rows, dtype=jnp.int32)
    peer_ids = jnp.arange(devices, dtype=jnp.int32)
    outgoing = jnp.minimum(sent_start[:, None] + slot_ids[None, :], tok_rows - 1).reshape(-1)
    parcels = jnp.take(qkv_rows, outgoing, axis=0).reshape(devices, slot_count, full_width)
    arrived = lax.all_to_all(parcels, "inner", split_axis=0, concat_axis=0, tiled=True)
    source = jnp.sum((taken_end[None, :] <= row_ids[:, None]).astype(jnp.int32), axis=1)
    is_source = source[:, None] == peer_ids[None, :]
    offset_in = row_ids - jnp.sum(jnp.where(is_source, taken_start[None, :], 0), axis=1)
    incoming = source * slot_count + offset_in
    owned_rows = jnp.take(arrived.reshape(devices * slot_count, full_width), incoming, axis=0)
    query_blocks = self_index * per_device + jnp.arange(per_device, dtype=jnp.int32)
    query_image, tile_row, tile_col = block_places(query_blocks, image_dims)
    within = jnp.arange(block_rows, dtype=jnp.int32)
    row_pos = (tile_row[:, None] * TR + within[None, :] // TC).reshape(-1)
    col_pos = (tile_col[:, None] * TC + within[None, :] % TC).reshape(-1)
    queries = rotate(owned_rows[:, :inner_width], row_pos, col_pos).reshape(tok_rows, H, HD)
    keys = rotate(owned_rows[:, inner_width : 2 * inner_width], row_pos, col_pos)
    key_value = jnp.stack([keys, owned_rows[:, 2 * inner_width :]])

    def absorb(softmax_state, key_piece, allowed):
        row_max, row_sum, summed = softmax_state
        visible = jnp.repeat(jnp.repeat(allowed, block_rows, axis=0), block_rows, axis=1)[
            :, None, :
        ]
        far_keys = key_piece[0].reshape(tok_rows, H, HD)
        far_values = key_piece[1].reshape(tok_rows, H, HD)
        scores = (
            jnp.einsum("qhd,khd->qhk", queries, far_keys, preferred_element_type=jnp.float32)
            * score_scale
        )
        scores = jnp.where(visible, scores, -1e30)
        new_max = jnp.maximum(row_max, jnp.max(scores, axis=2))
        weights = jnp.where(visible, jnp.exp(scores - new_max[:, :, None]), 0.0)
        rescale = jnp.exp(row_max - new_max)
        row_sum = row_sum * rescale + jnp.sum(weights, axis=2)
        summed = summed * rescale[:, :, None] + jnp.einsum(
            "qhk,khd->qhd",
            weights.astype(jnp.bfloat16),
            far_values,
            preferred_element_type=jnp.float32,
        )
        return (new_max, row_sum, summed)

    def visit(softmax_state, key_piece, source_dev):
        key_blocks = source_dev * per_device + jnp.arange(per_device, dtype=jnp.int32)
        key_image = block_places(key_blocks, image_dims)[0]
        offset = key_blocks[None, :] - query_blocks[:, None] + (MAXT - 1)
        mask_bits = jnp.take_along_axis(block_mask, jnp.clip(offset, 0, WIN - 1), axis=1)
        allowed = (
            (offset >= 0)
            & (offset < WIN)
            & (mask_bits == 1)
            & (query_image[:, None] == key_image[None, :])
            & (source_dev >= 0)
            & (source_dev < devices)
        )
        return absorb(softmax_state, key_piece, allowed)

    initial = (
        jnp.full((tok_rows, H), -1e30, jnp.float32),
        jnp.zeros((tok_rows, H), jnp.float32),
        jnp.zeros((tok_rows, H, HD), jnp.float32),
    )
    farthest = from_behind(key_value, "inner", -reach_count)
    softmax_state = visit(initial, farthest, self_index + reach_count)

    def one_way(hop_index, carry):
        key_piece, running = carry
        key_piece = from_behind(key_piece, "inner", 1)
        return (key_piece, visit(running, key_piece, self_index + reach_count - hop_index - 1))

    softmax_state = lax.fori_loop(0, 2 * reach_count, one_way, (farthest, softmax_state))[1]
    row_max, row_sum, summed = softmax_state
    attended = (summed / row_sum[:, :, None]).reshape(tok_rows, H * HD).astype(jnp.bfloat16)
    projected = jnp.dot(attended, out_weight, preferred_element_type=jnp.float32).astype(
        jnp.bfloat16
    )
    out_width = projected.shape[1]
    back_slots = jnp.minimum(taken_start[:, None] + slot_ids[None, :], tok_rows - 1).reshape(-1)
    returning = jnp.take(projected, back_slots, axis=0).reshape(devices, slot_count, out_width)
    returned = lax.all_to_all(returning, "inner", split_axis=0, concat_axis=0, tiled=True)
    target = jnp.sum((sent_end[None, :] <= row_ids[:, None]).astype(jnp.int32), axis=1)
    is_target = target[:, None] == peer_ids[None, :]
    offset_back = row_ids - jnp.sum(jnp.where(is_target, sent_start[None, :], 0), axis=1)
    return jnp.take(
        returned.reshape(devices * slot_count, out_width), target * slot_count + offset_back, axis=0
    )


ROWS = TR * TC
EXTRA = 16
HIDDEN = -1e30
MESH_ID = pl.DeviceIdType.MESH


def nt_dot(a, b):
    return lax.dot_general(a, b, (((1,), (1,)), ((), ())), preferred_element_type=jnp.float32)


def nn_dot(a, b):
    return jnp.dot(a, b, preferred_element_type=jnp.float32)


def iota(shape, dim):
    return lax.broadcasted_iota(jnp.int32, shape, dim)


def head_kernel(
    devices,
    qkv_ref,
    pair_ref,
    dims_ref,
    mask_ref,
    freq_ref,
    out_ref,
    q_out,
    k_out,
    q_in,
    k_in,
    v_in,
    tile_of,
    starts_ref,
    ends_ref,
    bias_ref,
    weights_ref,
    sum_ref,
    total_ref,
    done_ref,
    home_ref,
    send_sem,
    recv_sem,
    pass_send_sem,
    pass_recv_sem,
    back_send_sem,
    back_recv_sem,
):
    me = lax.axis_index("inner")
    group = lax.axis_index("group")
    chips = devices // 2
    chip = me // 2
    core = me % 2
    sibling = chip * 2 + (1 - core)
    first_chip = (chips - H) // 2
    head = chip - first_chip
    has_head = (head >= 0) & (head < H)

    def device(index):
        return (group, index)

    barrier = pltpu.get_barrier_semaphore()
    for hop in range(1, chips):
        pl.semaphore_signal(
            barrier, inc=1, device_id=device((chip ^ hop) * 2 + core), device_id_type=MESH_ID
        )
    pl.semaphore_signal(barrier, inc=1, device_id=device(sibling), device_id_type=MESH_ID)

    src = iota((devices, 128), 0)
    dst = iota((devices, 128), 1)
    pairs = pair_ref[...].astype(jnp.float32).astype(jnp.bfloat16)
    ends = nn_dot(pairs, jnp.where(src <= dst, 1.0, 0.0).astype(jnp.bfloat16))
    starts = nn_dot(pairs, jnp.where(src < dst, 1.0, 0.0).astype(jnp.bfloat16))
    wide = nn_dot(pairs, jnp.where(src == dst, 1.0, 0.0).astype(jnp.bfloat16))
    below = jnp.where(iota((devices, devices), 1) < iota((devices, devices), 0), 1.0, 0.0)
    column_starts = nn_dot(below.astype(jnp.bfloat16), wide.astype(jnp.bfloat16))
    starts_ref[...] = starts
    ends_ref[...] = ends
    row = iota((ROWS, 128), 0).astype(jnp.float32)
    lane = iota((ROWS, 128), 1)

    def one_hot(loader):
        low = starts_ref[pl.ds(loader, 1), :]
        high = ends_ref[pl.ds(loader, 1), :]
        return jnp.where((row >= low) & (row < high), 1.0, 0.0)

    heights = jnp.broadcast_to(dims_ref[0:1, :], (devices, devices)).astype(jnp.float32)
    widths = jnp.broadcast_to(dims_ref[1:2, :], (devices, devices)).astype(jnp.float32)
    spread = jnp.where(src == dst, 1.0, 0.0).astype(jnp.bfloat16)
    before = jnp.where(src < dst, 1.0, 0.0).astype(jnp.bfloat16)
    first_tile = nn_dot((heights * widths).astype(jnp.bfloat16), before)
    widths = nn_dot(widths.astype(jnp.bfloat16), spread)
    tile = src.astype(jnp.float32)
    image = jnp.sum(jnp.where(first_tile <= tile, 1.0, 0.0), axis=1, keepdims=True) - 1.0
    picked = jnp.where(dst.astype(jnp.float32) == image, 1.0, 0.0)
    local = tile[:, 0:1] - jnp.sum(picked * first_tile, axis=1, keepdims=True)
    across = jnp.maximum(jnp.sum(picked * widths, axis=1, keepdims=True), 1.0)
    tile_row = jnp.floor((local + 0.5) / across)
    tile_col = local - tile_row * across
    places = jnp.where(dst == 0, tile_row * TR, jnp.where(dst == 1, tile_col * TC, 0.0))
    picked_low = picked.astype(jnp.bfloat16)
    same_image = nn_dot(nt_dot(picked_low, picked_low).astype(jnp.bfloat16), spread)

    mine = one_hot(me)
    own_row = iota((devices, 128), 0) == me
    shift = jnp.sum(jnp.where(own_row, column_starts - starts, 0.0), axis=0, keepdims=True)
    within = row[:, 0:1] + jnp.sum(mine * shift, axis=1, keepdims=True)
    place = nn_dot(mine[:, 0:devices].astype(jnp.bfloat16), places.astype(jnp.bfloat16))
    line = jnp.floor(within * (1.0 / TC))
    row_pos = place[:, 0:1] + line
    col_pos = place[:, 1:2] + within - line * TC
    angle = jnp.where(lane < HD // 2, row_pos, col_pos) * freq_ref[0:1, :]
    leading = (lane % (HD // 2)) < HD // 4
    cosine = jnp.cos(angle)
    sine = jnp.where(leading, -1.0, 1.0) * jnp.sin(angle)

    def turn(values):
        ahead = pltpu.roll(values, HD - HD // 4, 1)
        behind = pltpu.roll(values, HD // 4, 1)
        return (values * cosine + jnp.where(leading, ahead, behind) * sine).astype(jnp.bfloat16)

    mask_row = jnp.concatenate(
        [mask_ref[...].astype(jnp.float32), jnp.zeros((1, 128 - WIN), jnp.float32)], axis=1
    )
    extra = jnp.where(iota((EXTRA, 128), 0) == me, mask_row, 0.0).astype(jnp.bfloat16)
    for h in range(H):
        at = h * HD
        q_out[h] = turn(qkv_ref[:, at : at + HD].astype(jnp.float32))
        at = (H + h) * HD
        k_out[h, 0:ROWS] = turn(qkv_ref[:, at : at + HD].astype(jnp.float32))
        k_out[h, ROWS : ROWS + EXTRA] = extra

    pl.semaphore_wait(barrier, chips)

    def value_block(h):
        return qkv_ref.at[:, pl.ds(pl.multiple_of((2 * H + h) * HD, HD), HD)]

    def parcel(kind, h, loader, slot, target):
        if kind == 0:
            source, dest = k_out.at[h], k_in.at[loader]
        elif kind == 1:
            source, dest = q_out.at[h], q_in.at[slot]
        else:
            source, dest = value_block(h), v_in.at[loader]
        return pltpu.make_async_remote_copy(
            src_ref=source,
            dst_ref=dest,
            send_sem=send_sem.at[kind, h],
            recv_sem=recv_sem.at[kind, slot],
            device_id=device(target),
            device_id_type=MESH_ID,
        )

    def relay(kind, slot):
        ref = k_in if kind == 0 else v_in
        block = ref.at[slot * 2 + core]
        return pltpu.make_async_remote_copy(
            src_ref=block,
            dst_ref=block,
            send_sem=pass_send_sem.at[kind, slot],
            recv_sem=pass_recv_sem.at[kind, slot],
            device_id=device(sibling),
            device_id_type=MESH_ID,
        )

    def relayed(kind, slot):
        ref = k_in if kind == 0 else v_in
        block = ref.at[slot * 2 + 1 - core]
        return pltpu.make_async_remote_copy(
            src_ref=block,
            dst_ref=block,
            send_sem=pass_send_sem.at[kind, slot],
            recv_sem=pass_recv_sem.at[kind, slot],
            device_id=device(sibling),
            device_id_type=MESH_ID,
        )

    def back(h, slot, target):
        return pltpu.make_async_remote_copy(
            src_ref=done_ref.at[slot],
            dst_ref=home_ref.at[h],
            send_sem=back_send_sem.at[slot],
            recv_sem=back_recv_sem.at[h],
            device_id=device(target),
            device_id_type=MESH_ID,
        )

    def each_target(action):
        for kind in range(3):
            for hop in range(1, chips):
                to_chip = chip ^ hop
                h = to_chip - first_chip

                @pl.when((h >= 0) & (h < H))
                def _():
                    action(parcel(kind, h, me, chip, to_chip * 2 + core))

    each_target(lambda copy: copy.start())

    @pl.when(has_head)
    def _():
        k_in[me] = k_out[head]
        q_in[chip] = q_out[head]
        v_in[me] = qkv_ref[:, pl.ds(pl.multiple_of((2 * H + head) * HD, HD), HD)]
        relay(0, chip).start()
        relay(2, chip).start()

        def make_tiles(loader, carry):
            tile_of[loader] = one_hot(loader).astype(jnp.bfloat16)
            return carry

        lax.fori_loop(0, devices, make_tiles, 0)
        for hop in range(1, chips):
            slot = chip ^ hop
            parcel(0, head, slot * 2 + core, slot, me).wait_recv()
            relay(0, slot).start()
        for hop in range(chips):
            relayed(0, chip ^ hop).wait_recv()

        bits = jnp.sum(k_in[:, ROWS : ROWS + EXTRA, :].astype(jnp.float32), axis=0)
        seen = jnp.zeros((EXTRA, 128), jnp.float32)
        apart = iota((EXTRA, 128), 1) - iota((EXTRA, 128), 0) + (MAXT - 1)
        for o in range(WIN):
            seen = seen + jnp.where(apart == o, bits[:, o : o + 1], 0.0)
        allowed = (seen > 0.5) & (same_image > 0.5)
        hidden = jnp.where(allowed, 0.0, HIDDEN).astype(jnp.bfloat16)
        bias_ref[...] = hidden

        factor = math.log2(math.e) / math.sqrt(HD)

        def score(hop, carry):
            slot = chip ^ hop

            @pl.when(hop > 0)
            def _():
                parcel(1, head, slot * 2 + core, slot, me).wait_recv()

            own_tile = tile_of[slot * 2 + core][:, 0:EXTRA]
            veil = nn_dot(own_tile, bias_ref[...]).astype(jnp.bfloat16)
            query = jnp.concatenate([q_in[slot], veil], axis=1)
            key = jnp.concatenate(
                [
                    k_in[:, 0:ROWS, :].reshape(devices * ROWS, HD),
                    tile_of[...].reshape(devices * ROWS, 128),
                ],
                axis=1,
            )
            scores = nt_dot(query, key)
            top = jnp.max(scores, axis=1, keepdims=True)
            weight = jnp.exp2((scores - top) * factor)
            sum_ref[slot] = jnp.broadcast_to(jnp.sum(weight, axis=1, keepdims=True), (ROWS, 128))
            weight = weight.astype(jnp.bfloat16)
            for c in range(chips):
                weights_ref[c, pl.ds(pl.multiple_of(slot * ROWS, ROWS), ROWS), :] = weight[
                    :, c * 2 * ROWS : (c + 1) * 2 * ROWS
                ]
            return carry

        lax.fori_loop(0, chips, score, 0)

        for hop in range(1, chips):
            slot = chip ^ hop
            parcel(2, head, slot * 2 + core, slot, me).wait_recv()
            relay(2, slot).start()

        total_ref[...] = jnp.zeros_like(total_ref)

        def mix(hop, carry):
            slot = chip ^ hop
            relayed(2, slot).wait_recv()
            value = v_in[pl.ds(slot * 2, 2)].reshape(2 * ROWS, HD)
            total_ref[...] += nn_dot(weights_ref[slot], value)
            return carry

        lax.fori_loop(0, chips, mix, 0)

        for hop in range(chips - 1, -1, -1):
            slot = chip ^ hop
            rows = pl.ds(pl.multiple_of(slot * ROWS, ROWS), ROWS)
            done_ref[slot] = (total_ref[rows, :] / sum_ref[slot]).astype(jnp.bfloat16)
            if hop:
                back(head, slot, slot * 2 + core).start()
            else:
                home_ref[head] = done_ref[slot]

        for hop in range(chips):
            relay(0, chip ^ hop).wait_send()
            relay(2, chip ^ hop).wait_send()
            if hop:
                back(head, chip ^ hop, (chip ^ hop) * 2 + core).wait_send()

    each_target(lambda copy: copy.wait_send())
    for h in range(H):

        @pl.when(head != h)
        def _():
            back(h, chip, me).wait_recv()

        out_ref[:, h * HD : (h + 1) * HD] = home_ref[h]


def by_head(qkv_rows, pair_counts, image_dims, block_mask, out_weight):
    devices = lax.axis_size("inner")
    chips = devices // 2
    low = jnp.bfloat16
    quarter = HD // 4
    lane = np.arange(HD) % quarter
    frequency = np.power(np.float32(10000.0), -lane.astype(np.float32) / np.float32(quarter))
    frequency = np.broadcast_to(frequency.astype(np.float32), (8, HD))
    attended = pl.pallas_call(
        functools.partial(head_kernel, devices),
        name="attend",
        out_shape=jax.ShapeDtypeStruct((ROWS, H * HD), low),
        in_specs=[pl.BlockSpec(memory_space=pltpu.VMEM)] * 5,
        out_specs=pl.BlockSpec(memory_space=pltpu.VMEM),
        scratch_shapes=[
            pltpu.VMEM((H, ROWS, HD), low),
            pltpu.VMEM((H, ROWS + EXTRA, HD), low),
            pltpu.VMEM((chips, ROWS, HD), low),
            pltpu.VMEM((devices, ROWS + EXTRA, HD), low),
            pltpu.VMEM((devices, ROWS, HD), low),
            pltpu.VMEM((devices, ROWS, 128), low),
            pltpu.VMEM((devices, 128), jnp.float32),
            pltpu.VMEM((devices, 128), jnp.float32),
            pltpu.VMEM((EXTRA, 128), low),
            pltpu.VMEM((chips, chips * ROWS, 2 * ROWS), low),
            pltpu.VMEM((chips, ROWS, 128), jnp.float32),
            pltpu.VMEM((chips * ROWS, HD), jnp.float32),
            pltpu.VMEM((chips, ROWS, HD), low),
            pltpu.VMEM((H, ROWS, HD), low),
            pltpu.SemaphoreType.DMA((3, H)),
            pltpu.SemaphoreType.DMA((3, chips)),
            pltpu.SemaphoreType.DMA((3, chips)),
            pltpu.SemaphoreType.DMA((3, chips)),
            pltpu.SemaphoreType.DMA((chips,)),
            pltpu.SemaphoreType.DMA((H,)),
        ],
        compiler_params=pltpu.CompilerParams(
            collective_id=0, has_side_effects=True, vmem_limit_bytes=48 * 1024 * 1024
        ),
        cost_estimate=pl.CostEstimate(
            flops=2 * 1024 * 2048 * 384, bytes_accessed=1 << 20, transcendentals=1024 * 2048
        ),
    )(qkv_rows, pair_counts, image_dims, block_mask, jnp.asarray(frequency))
    return jnp.dot(attended, out_weight, preferred_element_type=jnp.float32).astype(low)


def solution(mesh):
    body = by_head if mesh.shape["inner"] == EXTRA else shards
    in_specs = (
        P(("group", "inner"), None),
        P("group", None),
        P(None, "group"),
        P(("group", "inner"), None),
        P(),
    )
    out_specs = P(("group", "inner"), None)
    return jax.shard_map(body, mesh=mesh, in_specs=in_specs, out_specs=out_specs, check_vma=False)
```

```python
import functools
import math

import jax
import jax.numpy as jnp
from jax import lax
from jax.experimental import pallas as pl
from jax.experimental.pallas import tpu as pltpu
from jax.sharding import PartitionSpec as P

H = 6
HD = 128
TR = 8
TC = 16
SPAN = 4
MAXT = 4
WIN = 7


def running(counts):
    ids = jnp.arange(counts.shape[0], dtype=jnp.int32)
    return jnp.sum(jnp.where(ids[:, None] <= ids[None, :], counts[:, None], 0), axis=0)


def from_behind(value, axis, steps):
    count = lax.axis_size(axis)
    pairs = [(source, (source + steps) % count) for source in range(count)]
    return lax.ppermute(value, axis, pairs)


def block_places(blocks, image_dims):
    heights = image_dims[0]
    widths = image_dims[1]
    tile_count = heights * widths
    starts = running(tile_count) - tile_count
    inside = (starts[None, :] <= blocks[:, None]).astype(jnp.int32)
    image_id = jnp.sum(inside, axis=1) - 1
    picked = jnp.arange(starts.shape[0], dtype=jnp.int32)[None, :] == image_id[:, None]
    first_block = jnp.sum(jnp.where(picked, starts[None, :], 0), axis=1)
    across = jnp.maximum(jnp.sum(jnp.where(picked, widths[None, :], 0), axis=1), 1)
    local_tile = blocks - first_block
    return (image_id, local_tile // across, local_tile % across)


def rotate(rows_in, row_pos, col_pos):
    count = rows_in.shape[0]
    quarter = HD // 4
    frequency = 10000.0 ** (-jnp.arange(quarter, dtype=jnp.float32) / quarter)
    angles = jnp.stack(
        [
            row_pos.astype(jnp.float32)[:, None] * frequency[None, :],
            col_pos.astype(jnp.float32)[:, None] * frequency[None, :],
        ],
        axis=1,
    )
    cosine = jnp.cos(angles)[:, None, :, :]
    sine_part = jnp.sin(angles)[:, None, :, :]
    split_rows = rows_in.astype(jnp.float32).reshape(count, H, 2, 2, quarter)
    leading = split_rows[:, :, :, 0, :]
    trailing = split_rows[:, :, :, 1, :]
    turned = jnp.stack(
        [leading * cosine - trailing * sine_part, trailing * cosine + leading * sine_part], axis=3
    )
    return turned.reshape(count, H * HD).astype(jnp.bfloat16)


def shards(qkv_rows, pair_counts, image_dims, block_mask, out_weight):
    devices = lax.axis_size("inner")
    self_index = lax.axis_index("inner")
    tok_rows = qkv_rows.shape[0]
    full_width = qkv_rows.shape[1]
    inner_width = full_width // 3
    slot_count = 2 * tok_rows // devices
    block_rows = TR * TC
    per_device = tok_rows // block_rows
    reach_count = (SPAN * tok_rows - block_rows + tok_rows - 1) // tok_rows
    score_scale = 1.0 / math.sqrt(HD)
    sent_counts = lax.dynamic_index_in_dim(pair_counts, self_index, 0, keepdims=False)
    taken_counts = lax.dynamic_index_in_dim(pair_counts, self_index, 1, keepdims=False)
    sent_end = running(sent_counts)
    sent_start = sent_end - sent_counts
    taken_end = running(taken_counts)
    taken_start = taken_end - taken_counts
    slot_ids = jnp.arange(slot_count, dtype=jnp.int32)
    row_ids = jnp.arange(tok_rows, dtype=jnp.int32)
    peer_ids = jnp.arange(devices, dtype=jnp.int32)
    outgoing = jnp.minimum(sent_start[:, None] + slot_ids[None, :], tok_rows - 1).reshape(-1)
    parcels = jnp.take(qkv_rows, outgoing, axis=0).reshape(devices, slot_count, full_width)
    arrived = lax.all_to_all(parcels, "inner", split_axis=0, concat_axis=0, tiled=True)
    source = jnp.sum((taken_end[None, :] <= row_ids[:, None]).astype(jnp.int32), axis=1)
    is_source = source[:, None] == peer_ids[None, :]
    offset_in = row_ids - jnp.sum(jnp.where(is_source, taken_start[None, :], 0), axis=1)
    incoming = source * slot_count + offset_in
    owned_rows = jnp.take(arrived.reshape(devices * slot_count, full_width), incoming, axis=0)
    query_blocks = self_index * per_device + jnp.arange(per_device, dtype=jnp.int32)
    query_image, tile_row, tile_col = block_places(query_blocks, image_dims)
    within = jnp.arange(block_rows, dtype=jnp.int32)
    row_pos = (tile_row[:, None] * TR + within[None, :] // TC).reshape(-1)
    col_pos = (tile_col[:, None] * TC + within[None, :] % TC).reshape(-1)
    queries = rotate(owned_rows[:, :inner_width], row_pos, col_pos).reshape(tok_rows, H, HD)
    keys = rotate(owned_rows[:, inner_width : 2 * inner_width], row_pos, col_pos)
    key_value = jnp.stack([keys, owned_rows[:, 2 * inner_width :]])

    def absorb(softmax_state, key_piece, allowed):
        row_max, row_sum, summed = softmax_state
        visible = jnp.repeat(jnp.repeat(allowed, block_rows, axis=0), block_rows, axis=1)[
            :, None, :
        ]
        far_keys = key_piece[0].reshape(tok_rows, H, HD)
        far_values = key_piece[1].reshape(tok_rows, H, HD)
        scores = (
            jnp.einsum("qhd,khd->qhk", queries, far_keys, preferred_element_type=jnp.float32)
            * score_scale
        )
        scores = jnp.where(visible, scores, -1e30)
        new_max = jnp.maximum(row_max, jnp.max(scores, axis=2))
        weights = jnp.where(visible, jnp.exp(scores - new_max[:, :, None]), 0.0)
        rescale = jnp.exp(row_max - new_max)
        row_sum = row_sum * rescale + jnp.sum(weights, axis=2)
        summed = summed * rescale[:, :, None] + jnp.einsum(
            "qhk,khd->qhd",
            weights.astype(jnp.bfloat16),
            far_values,
            preferred_element_type=jnp.float32,
        )
        return (new_max, row_sum, summed)

    def visit(softmax_state, key_piece, source_dev):
        key_blocks = source_dev * per_device + jnp.arange(per_device, dtype=jnp.int32)
        key_image = block_places(key_blocks, image_dims)[0]
        offset = key_blocks[None, :] - query_blocks[:, None] + (MAXT - 1)
        mask_bits = jnp.take_along_axis(block_mask, jnp.clip(offset, 0, WIN - 1), axis=1)
        allowed = (
            (offset >= 0)
            & (offset < WIN)
            & (mask_bits == 1)
            & (query_image[:, None] == key_image[None, :])
            & (source_dev >= 0)
            & (source_dev < devices)
        )
        return absorb(softmax_state, key_piece, allowed)

    initial = (
        jnp.full((tok_rows, H), -1e30, jnp.float32),
        jnp.zeros((tok_rows, H), jnp.float32),
        jnp.zeros((tok_rows, H, HD), jnp.float32),
    )
    farthest = from_behind(key_value, "inner", -reach_count)
    softmax_state = visit(initial, farthest, self_index + reach_count)

    def one_way(hop_index, carry):
        key_piece, running = carry
        key_piece = from_behind(key_piece, "inner", 1)
        return (key_piece, visit(running, key_piece, self_index + reach_count - hop_index - 1))

    softmax_state = lax.fori_loop(0, 2 * reach_count, one_way, (farthest, softmax_state))[1]
    row_max, row_sum, summed = softmax_state
    attended = (summed / row_sum[:, :, None]).reshape(tok_rows, H * HD).astype(jnp.bfloat16)
    projected = jnp.dot(attended, out_weight, preferred_element_type=jnp.float32).astype(
        jnp.bfloat16
    )
    out_width = projected.shape[1]
    back_slots = jnp.minimum(taken_start[:, None] + slot_ids[None, :], tok_rows - 1).reshape(-1)
    returning = jnp.take(projected, back_slots, axis=0).reshape(devices, slot_count, out_width)
    returned = lax.all_to_all(returning, "inner", split_axis=0, concat_axis=0, tiled=True)
    target = jnp.sum((sent_end[None, :] <= row_ids[:, None]).astype(jnp.int32), axis=1)
    is_target = target[:, None] == peer_ids[None, :]
    offset_back = row_ids - jnp.sum(jnp.where(is_target, sent_start[None, :], 0), axis=1)
    return jnp.take(
        returned.reshape(devices * slot_count, out_width), target * slot_count + offset_back, axis=0
    )


ROWS = TR * TC
EXTRA = 16
HIDDEN = -1e30
MESH_ID = pl.DeviceIdType.MESH


def nt_dot(a, b):
    return lax.dot_general(a, b, (((1,), (1,)), ((), ())), preferred_element_type=jnp.float32)


def nn_dot(a, b):
    return jnp.dot(a, b, preferred_element_type=jnp.float32)


def iota(shape, dim):
    return lax.broadcasted_iota(jnp.int32, shape, dim)


def head_kernel(
    devices,
    qkv_hbm,
    pair_hbm,
    dims_hbm,
    mask_hbm,
    out_ref,
    qkv_ref,
    pair_ref,
    dims_ref,
    mask_ref,
    load_sem,
    q_out,
    k_out,
    v_out,
    q_in,
    k_in,
    v_in,
    tile_of,
    starts_ref,
    ends_ref,
    bias_ref,
    done_ref,
    home_ref,
    send_sem,
    recv_sem,
    pass_send_sem,
    pass_recv_sem,
    back_send_sem,
    back_recv_sem,
):
    me = lax.axis_index("inner")
    group = lax.axis_index("group")
    chips = devices // 2
    chip = me // 2
    core = me % 2
    sibling = chip * 2 + (1 - core)
    first_chip = (chips - H) // 2
    head = chip - first_chip
    has_head = (head >= 0) & (head < H)

    def device(index):
        return (group, index)

    barrier = pltpu.get_barrier_semaphore()
    for hop in range(1, chips):
        pl.semaphore_signal(
            barrier, inc=1, device_id=device((chip ^ hop) * 2 + core), device_id_type=MESH_ID
        )
    pl.semaphore_signal(barrier, inc=1, device_id=device(sibling), device_id_type=MESH_ID)

    inner_width = H * HD

    def load(source, dest, index):
        copy = pltpu.make_async_copy(source, dest, load_sem.at[index])
        copy.start()
        return copy

    def columns(part):
        at = part * inner_width
        return qkv_hbm.at[:, at : at + inner_width], qkv_ref.at[:, at : at + inner_width]

    load_pair = load(pair_hbm, pair_ref, 0)
    load_dims = load(dims_hbm, dims_ref, 1)
    load_mask = load(mask_hbm, mask_ref, 2)
    load_key = load(*columns(1), 3)
    load_value = load(*columns(2), 4)
    load_query = load(*columns(0), 5)

    row = iota((ROWS, 128), 0).astype(jnp.float32)
    lane = iota((ROWS, 128), 1)
    quarter = HD // 4
    half = HD // 2
    power = (lane % quarter).astype(jnp.float32) * (-math.log(10000.0) / quarter)
    upper = iota((ROWS, 128), 0) < half
    angle = jnp.where(upper, row, row - half) * jnp.exp(power)
    leading = (lane % half) < quarter
    paired = upper == (lane < half)
    cosine_table = jnp.where(paired, jnp.cos(angle), 0.0)
    sine_table = jnp.where(paired, jnp.where(leading, -1.0, 1.0) * jnp.sin(angle), 0.0)
    table = jnp.concatenate([cosine_table, sine_table], axis=1)
    high_part = table.astype(jnp.bfloat16)
    left_over = table - high_part.astype(jnp.float32)
    mid_part = left_over.astype(jnp.bfloat16)
    low_part = (left_over - mid_part.astype(jnp.float32)).astype(jnp.bfloat16)
    load_pair.wait()
    load_dims.wait()
    load_mask.wait()

    src = iota((devices, 128), 0)
    dst = iota((devices, 128), 1)
    pairs = pair_ref[...].astype(jnp.float32).astype(jnp.bfloat16)
    ends = nn_dot(pairs, jnp.where(src <= dst, 1.0, 0.0).astype(jnp.bfloat16))
    starts = nn_dot(pairs, jnp.where(src < dst, 1.0, 0.0).astype(jnp.bfloat16))
    wide = nn_dot(pairs, jnp.where(src == dst, 1.0, 0.0).astype(jnp.bfloat16))
    below = jnp.where(iota((devices, devices), 1) < iota((devices, devices), 0), 1.0, 0.0)
    column_starts = nn_dot(below.astype(jnp.bfloat16), wide.astype(jnp.bfloat16))
    starts_ref[...] = starts
    ends_ref[...] = ends

    def one_hot(loader):
        low = starts_ref[pl.ds(loader, 1), :]
        high = ends_ref[pl.ds(loader, 1), :]
        return jnp.where((row >= low) & (row < high), 1.0, 0.0)

    heights = jnp.broadcast_to(dims_ref[0:1, :], (devices, devices)).astype(jnp.float32)
    widths = jnp.broadcast_to(dims_ref[1:2, :], (devices, devices)).astype(jnp.float32)
    spread = jnp.where(src == dst, 1.0, 0.0).astype(jnp.bfloat16)
    before = jnp.where(src < dst, 1.0, 0.0).astype(jnp.bfloat16)
    first_tile = nn_dot((heights * widths).astype(jnp.bfloat16), before)
    widths = nn_dot(widths.astype(jnp.bfloat16), spread)
    tile = src.astype(jnp.float32)
    image = jnp.sum(jnp.where(first_tile <= tile, 1.0, 0.0), axis=1, keepdims=True) - 1.0
    picked = jnp.where(dst.astype(jnp.float32) == image, 1.0, 0.0)
    local = tile[:, 0:1] - jnp.sum(picked * first_tile, axis=1, keepdims=True)
    across = jnp.maximum(jnp.sum(picked * widths, axis=1, keepdims=True), 1.0)
    tile_row = jnp.floor((local + 0.5) / across)
    tile_col = local - tile_row * across
    places = jnp.where(dst == 0, tile_row * TR, jnp.where(dst == 1, tile_col * TC, 0.0))
    picked_low = picked.astype(jnp.bfloat16)
    same_image = nn_dot(nt_dot(picked_low, picked_low).astype(jnp.bfloat16), spread)

    mine = one_hot(me)
    own_row = iota((devices, 128), 0) == me
    shift = jnp.sum(jnp.where(own_row, column_starts - starts, 0.0), axis=0, keepdims=True)
    within = row[:, 0:1] + jnp.sum(mine * shift, axis=1, keepdims=True)
    place = nn_dot(mine[:, 0:devices].astype(jnp.bfloat16), places.astype(jnp.bfloat16))
    line = jnp.floor(within * (1.0 / TC))
    row_pos = place[:, 0:1] + line
    col_pos = place[:, 1:2] + within - line * TC
    lane_at = lane.astype(jnp.float32)
    chosen = (lane_at == row_pos) | (lane_at == col_pos + half)
    chosen = jnp.where(chosen, 1.0, 0.0).astype(jnp.bfloat16)
    circle = nn_dot(chosen, high_part) + (nn_dot(chosen, mid_part) + nn_dot(chosen, low_part))
    cosine = circle[:, 0:HD]
    sine = circle[:, HD : 2 * HD]

    def turn(values):
        ahead = pltpu.roll(values, HD - HD // 4, 1)
        behind = pltpu.roll(values, HD // 4, 1)
        return (values * cosine + jnp.where(leading, ahead, behind) * sine).astype(jnp.bfloat16)

    mask_row = jnp.concatenate(
        [mask_ref[...].astype(jnp.float32), jnp.zeros((1, 128 - WIN), jnp.float32)], axis=1
    )
    extra = jnp.where(iota((EXTRA, 128), 0) == me, mask_row, 0.0).astype(jnp.bfloat16)
    load_key.wait()
    for h in range(H):
        at = (H + h) * HD
        k_out[h, 0:ROWS] = turn(qkv_ref[:, at : at + HD].astype(jnp.float32))
        k_out[h, ROWS : ROWS + EXTRA] = extra

    pl.semaphore_wait(barrier, chips)

    def parcel(kind, h, loader, slot, target):
        if kind == 0:
            source, dest = k_out.at[h], k_in.at[loader]
        elif kind == 1:
            source, dest = q_out.at[h], q_in.at[slot]
        else:
            source, dest = v_out.at[h], v_in.at[loader]
        return pltpu.make_async_remote_copy(
            src_ref=source,
            dst_ref=dest,
            send_sem=send_sem.at[kind, h],
            recv_sem=recv_sem.at[kind, slot],
            device_id=device(target),
            device_id_type=MESH_ID,
        )

    def relay(kind, slot):
        ref = k_in if kind == 0 else v_in
        block = ref.at[slot * 2 + core]
        return pltpu.make_async_remote_copy(
            src_ref=block,
            dst_ref=block,
            send_sem=pass_send_sem.at[kind, slot],
            recv_sem=pass_recv_sem.at[kind, slot],
            device_id=device(sibling),
            device_id_type=MESH_ID,
        )

    def relayed(kind, slot):
        ref = k_in if kind == 0 else v_in
        block = ref.at[slot * 2 + 1 - core]
        return pltpu.make_async_remote_copy(
            src_ref=block,
            dst_ref=block,
            send_sem=pass_send_sem.at[kind, slot],
            recv_sem=pass_recv_sem.at[kind, slot],
            device_id=device(sibling),
            device_id_type=MESH_ID,
        )

    def back(h, slot, target):
        return pltpu.make_async_remote_copy(
            src_ref=done_ref.at[slot],
            dst_ref=home_ref.at[h],
            send_sem=back_send_sem.at[slot],
            recv_sem=back_recv_sem.at[h],
            device_id=device(target),
            device_id_type=MESH_ID,
        )

    def each_target(kind, action):
        for hop in range(chips - 1, 0, -1):
            to_chip = chip ^ hop
            h = to_chip - first_chip

            @pl.when((h >= 0) & (h < H))
            def _():
                action(parcel(kind, h, me, chip, to_chip * 2 + core))

    each_target(0, lambda copy: copy.start())

    @pl.when(has_head)
    def _():
        k_in[me] = k_out[head]
        relay(0, chip).start()

    load_value.wait()
    for h in range(H):
        at = (2 * H + h) * HD
        v_out[h] = qkv_ref[:, at : at + HD].T
    each_target(2, lambda copy: copy.start())

    @pl.when(has_head)
    def _():
        v_in[me] = v_out[head]
        relay(2, chip).start()

    load_query.wait()
    for h in range(H):
        at = h * HD
        q_out[h] = turn(qkv_ref[:, at : at + HD].astype(jnp.float32))
    each_target(1, lambda copy: copy.start())

    @pl.when(has_head)
    def _():
        q_in[chip] = q_out[head]

        def make_tiles(loader, carry):
            tile_of[loader] = one_hot(loader).astype(jnp.bfloat16)
            return carry

        lax.fori_loop(0, devices, make_tiles, 0)
        for hop in range(1, chips):
            slot = chip ^ hop
            parcel(0, head, slot * 2 + core, slot, me).wait_recv()
            relay(0, slot).start()
        for hop in range(1, chips):
            slot = chip ^ hop
            parcel(2, head, slot * 2 + core, slot, me).wait_recv()
            relay(2, slot).start()
        for hop in range(chips):
            relayed(0, chip ^ hop).wait_recv()
        for hop in range(chips):
            relayed(2, chip ^ hop).wait_recv()

        bits = jnp.sum(k_in[:, ROWS : ROWS + EXTRA, :].astype(jnp.float32), axis=0)
        seen = jnp.zeros((EXTRA, 128), jnp.float32)
        apart = iota((EXTRA, 128), 1) - iota((EXTRA, 128), 0) + (MAXT - 1)
        for o in range(WIN):
            seen = seen + jnp.where(apart == o, bits[:, o : o + 1], 0.0)
        allowed = (seen > 0.5) & (same_image > 0.5)
        hidden = jnp.where(allowed, 0.0, HIDDEN).astype(jnp.bfloat16)
        bias_ref[...] = hidden

        factor = math.log2(math.e) / math.sqrt(HD)

        def score(hop, carry):
            slot = chip ^ hop

            @pl.when(hop > 0)
            def _():
                parcel(1, head, slot * 2 + core, slot, me).wait_recv()

            own_tile = tile_of[slot * 2 + core][:, 0:EXTRA]
            veil = nn_dot(own_tile, bias_ref[...]).astype(jnp.bfloat16)
            query = jnp.concatenate([q_in[slot], veil], axis=1)
            key = jnp.concatenate(
                [
                    k_in[:, 0:ROWS, :].reshape(devices * ROWS, HD),
                    tile_of[...].reshape(devices * ROWS, 128),
                ],
                axis=1,
            )
            scores = nt_dot(key, query)
            top = jnp.max(scores, axis=0, keepdims=True)
            weight = jnp.exp2((scores - top) * factor)
            row_sum = jnp.sum(weight, axis=0, keepdims=True)
            value = jnp.concatenate([v_in[d] for d in range(devices)], axis=1)
            mixed = nn_dot(value, weight.astype(jnp.bfloat16)) / row_sum
            done_ref[slot] = mixed.T.astype(jnp.bfloat16)

            @pl.when(hop > 0)
            def _():
                back(head, slot, slot * 2 + core).start()

            return carry

        lax.fori_loop(0, chips, score, 0)
        home_ref[head] = done_ref[chip]

        for hop in range(chips):
            relay(0, chip ^ hop).wait_send()
            relay(2, chip ^ hop).wait_send()
            if hop:
                back(head, chip ^ hop, (chip ^ hop) * 2 + core).wait_send()

    for kind in range(3):
        each_target(kind, lambda copy: copy.wait_send())
    for h in range(H):

        @pl.when(head != h)
        def _():
            back(h, chip, me).wait_recv()

        out_ref[:, h * HD : (h + 1) * HD] = home_ref[h]


def by_head(qkv_rows, pair_counts, image_dims, block_mask, out_weight):
    devices = lax.axis_size("inner")
    chips = devices // 2
    low = jnp.bfloat16
    attended = pl.pallas_call(
        functools.partial(head_kernel, devices),
        name="attend",
        out_shape=jax.ShapeDtypeStruct((ROWS, H * HD), low),
        in_specs=[pl.BlockSpec(memory_space=pltpu.HBM)] * 4,
        out_specs=pl.BlockSpec(memory_space=pltpu.VMEM),
        scratch_shapes=[
            pltpu.VMEM(qkv_rows.shape, low),
            pltpu.VMEM(pair_counts.shape, jnp.int32),
            pltpu.VMEM(image_dims.shape, jnp.int32),
            pltpu.VMEM(block_mask.shape, jnp.int32),
            pltpu.SemaphoreType.DMA((6,)),
            pltpu.VMEM((H, ROWS, HD), low),
            pltpu.VMEM((H, ROWS + EXTRA, HD), low),
            pltpu.VMEM((H, HD, ROWS), low),
            pltpu.VMEM((chips, ROWS, HD), low),
            pltpu.VMEM((devices, ROWS + EXTRA, HD), low),
            pltpu.VMEM((devices, ROWS, HD), low),
            pltpu.VMEM((devices, ROWS, 128), low),
            pltpu.VMEM((devices, 128), jnp.float32),
            pltpu.VMEM((devices, 128), jnp.float32),
            pltpu.VMEM((EXTRA, 128), low),
            pltpu.VMEM((chips, ROWS, HD), low),
            pltpu.VMEM((H, ROWS, HD), low),
            pltpu.SemaphoreType.DMA((3, H)),
            pltpu.SemaphoreType.DMA((3, chips)),
            pltpu.SemaphoreType.DMA((3, chips)),
            pltpu.SemaphoreType.DMA((3, chips)),
            pltpu.SemaphoreType.DMA((chips,)),
            pltpu.SemaphoreType.DMA((H,)),
        ],
        compiler_params=pltpu.CompilerParams(
            collective_id=0, has_side_effects=True, vmem_limit_bytes=48 * 1024 * 1024
        ),
        cost_estimate=pl.CostEstimate(
            flops=2 * 1024 * 2048 * 384, bytes_accessed=1 << 20, transcendentals=1024 * 2048
        ),
    )(qkv_rows, pair_counts, image_dims, block_mask)
    return jnp.dot(attended, out_weight, preferred_element_type=jnp.float32).astype(low)


def solution(mesh):
    body = by_head if mesh.shape["inner"] == EXTRA else shards
    in_specs = (
        P(("group", "inner"), None),
        P("group", None),
        P(None, "group"),
        P(("group", "inner"), None),
        P(),
    )
    out_specs = P(("group", "inner"), None)
    return jax.shard_map(body, mesh=mesh, in_specs=in_specs, out_specs=out_specs, check_vma=False)
```

```python
import functools
import math

import jax
import jax.numpy as jnp
from jax import lax
from jax.experimental import pallas as pl
from jax.experimental.pallas import tpu as pltpu
from jax.sharding import PartitionSpec as P

H = 6
HD = 128
TR = 8
TC = 16
SPAN = 4
MAXT = 4
WIN = 7


def running(counts):
    ids = jnp.arange(counts.shape[0], dtype=jnp.int32)
    return jnp.sum(jnp.where(ids[:, None] <= ids[None, :], counts[:, None], 0), axis=0)


def from_behind(value, axis, steps):
    count = lax.axis_size(axis)
    pairs = [(source, (source + steps) % count) for source in range(count)]
    return lax.ppermute(value, axis, pairs)


def block_places(blocks, image_dims):
    heights = image_dims[0]
    widths = image_dims[1]
    tile_count = heights * widths
    starts = running(tile_count) - tile_count
    inside = (starts[None, :] <= blocks[:, None]).astype(jnp.int32)
    image_id = jnp.sum(inside, axis=1) - 1
    picked = jnp.arange(starts.shape[0], dtype=jnp.int32)[None, :] == image_id[:, None]
    first_block = jnp.sum(jnp.where(picked, starts[None, :], 0), axis=1)
    across = jnp.maximum(jnp.sum(jnp.where(picked, widths[None, :], 0), axis=1), 1)
    local_tile = blocks - first_block
    return (image_id, local_tile // across, local_tile % across)


def rotate(rows_in, row_pos, col_pos):
    count = rows_in.shape[0]
    quarter = HD // 4
    frequency = 10000.0 ** (-jnp.arange(quarter, dtype=jnp.float32) / quarter)
    angles = jnp.stack(
        [
            row_pos.astype(jnp.float32)[:, None] * frequency[None, :],
            col_pos.astype(jnp.float32)[:, None] * frequency[None, :],
        ],
        axis=1,
    )
    cosine = jnp.cos(angles)[:, None, :, :]
    sine_part = jnp.sin(angles)[:, None, :, :]
    split_rows = rows_in.astype(jnp.float32).reshape(count, H, 2, 2, quarter)
    leading = split_rows[:, :, :, 0, :]
    trailing = split_rows[:, :, :, 1, :]
    turned = jnp.stack(
        [leading * cosine - trailing * sine_part, trailing * cosine + leading * sine_part], axis=3
    )
    return turned.reshape(count, H * HD).astype(jnp.bfloat16)


def shards(qkv_rows, pair_counts, image_dims, block_mask, out_weight):
    devices = lax.axis_size("inner")
    self_index = lax.axis_index("inner")
    tok_rows = qkv_rows.shape[0]
    full_width = qkv_rows.shape[1]
    inner_width = full_width // 3
    slot_count = 2 * tok_rows // devices
    block_rows = TR * TC
    per_device = tok_rows // block_rows
    reach_count = (SPAN * tok_rows - block_rows + tok_rows - 1) // tok_rows
    score_scale = 1.0 / math.sqrt(HD)
    sent_counts = lax.dynamic_index_in_dim(pair_counts, self_index, 0, keepdims=False)
    taken_counts = lax.dynamic_index_in_dim(pair_counts, self_index, 1, keepdims=False)
    sent_end = running(sent_counts)
    sent_start = sent_end - sent_counts
    taken_end = running(taken_counts)
    taken_start = taken_end - taken_counts
    slot_ids = jnp.arange(slot_count, dtype=jnp.int32)
    row_ids = jnp.arange(tok_rows, dtype=jnp.int32)
    peer_ids = jnp.arange(devices, dtype=jnp.int32)
    outgoing = jnp.minimum(sent_start[:, None] + slot_ids[None, :], tok_rows - 1).reshape(-1)
    parcels = jnp.take(qkv_rows, outgoing, axis=0).reshape(devices, slot_count, full_width)
    arrived = lax.all_to_all(parcels, "inner", split_axis=0, concat_axis=0, tiled=True)
    source = jnp.sum((taken_end[None, :] <= row_ids[:, None]).astype(jnp.int32), axis=1)
    is_source = source[:, None] == peer_ids[None, :]
    offset_in = row_ids - jnp.sum(jnp.where(is_source, taken_start[None, :], 0), axis=1)
    incoming = source * slot_count + offset_in
    owned_rows = jnp.take(arrived.reshape(devices * slot_count, full_width), incoming, axis=0)
    query_blocks = self_index * per_device + jnp.arange(per_device, dtype=jnp.int32)
    query_image, tile_row, tile_col = block_places(query_blocks, image_dims)
    within = jnp.arange(block_rows, dtype=jnp.int32)
    row_pos = (tile_row[:, None] * TR + within[None, :] // TC).reshape(-1)
    col_pos = (tile_col[:, None] * TC + within[None, :] % TC).reshape(-1)
    queries = rotate(owned_rows[:, :inner_width], row_pos, col_pos).reshape(tok_rows, H, HD)
    keys = rotate(owned_rows[:, inner_width : 2 * inner_width], row_pos, col_pos)
    key_value = jnp.stack([keys, owned_rows[:, 2 * inner_width :]])

    def absorb(softmax_state, key_piece, allowed):
        row_max, row_sum, summed = softmax_state
        visible = jnp.repeat(jnp.repeat(allowed, block_rows, axis=0), block_rows, axis=1)[
            :, None, :
        ]
        far_keys = key_piece[0].reshape(tok_rows, H, HD)
        far_values = key_piece[1].reshape(tok_rows, H, HD)
        scores = (
            jnp.einsum("qhd,khd->qhk", queries, far_keys, preferred_element_type=jnp.float32)
            * score_scale
        )
        scores = jnp.where(visible, scores, -1e30)
        new_max = jnp.maximum(row_max, jnp.max(scores, axis=2))
        weights = jnp.where(visible, jnp.exp(scores - new_max[:, :, None]), 0.0)
        rescale = jnp.exp(row_max - new_max)
        row_sum = row_sum * rescale + jnp.sum(weights, axis=2)
        summed = summed * rescale[:, :, None] + jnp.einsum(
            "qhk,khd->qhd",
            weights.astype(jnp.bfloat16),
            far_values,
            preferred_element_type=jnp.float32,
        )
        return (new_max, row_sum, summed)

    def visit(softmax_state, key_piece, source_dev):
        key_blocks = source_dev * per_device + jnp.arange(per_device, dtype=jnp.int32)
        key_image = block_places(key_blocks, image_dims)[0]
        offset = key_blocks[None, :] - query_blocks[:, None] + (MAXT - 1)
        mask_bits = jnp.take_along_axis(block_mask, jnp.clip(offset, 0, WIN - 1), axis=1)
        allowed = (
            (offset >= 0)
            & (offset < WIN)
            & (mask_bits == 1)
            & (query_image[:, None] == key_image[None, :])
            & (source_dev >= 0)
            & (source_dev < devices)
        )
        return absorb(softmax_state, key_piece, allowed)

    initial = (
        jnp.full((tok_rows, H), -1e30, jnp.float32),
        jnp.zeros((tok_rows, H), jnp.float32),
        jnp.zeros((tok_rows, H, HD), jnp.float32),
    )
    farthest = from_behind(key_value, "inner", -reach_count)
    softmax_state = visit(initial, farthest, self_index + reach_count)

    def one_way(hop_index, carry):
        key_piece, running = carry
        key_piece = from_behind(key_piece, "inner", 1)
        return (key_piece, visit(running, key_piece, self_index + reach_count - hop_index - 1))

    softmax_state = lax.fori_loop(0, 2 * reach_count, one_way, (farthest, softmax_state))[1]
    row_max, row_sum, summed = softmax_state
    attended = (summed / row_sum[:, :, None]).reshape(tok_rows, H * HD).astype(jnp.bfloat16)
    projected = jnp.dot(attended, out_weight, preferred_element_type=jnp.float32).astype(
        jnp.bfloat16
    )
    out_width = projected.shape[1]
    back_slots = jnp.minimum(taken_start[:, None] + slot_ids[None, :], tok_rows - 1).reshape(-1)
    returning = jnp.take(projected, back_slots, axis=0).reshape(devices, slot_count, out_width)
    returned = lax.all_to_all(returning, "inner", split_axis=0, concat_axis=0, tiled=True)
    target = jnp.sum((sent_end[None, :] <= row_ids[:, None]).astype(jnp.int32), axis=1)
    is_target = target[:, None] == peer_ids[None, :]
    offset_back = row_ids - jnp.sum(jnp.where(is_target, sent_start[None, :], 0), axis=1)
    return jnp.take(
        returned.reshape(devices * slot_count, out_width), target * slot_count + offset_back, axis=0
    )


ROWS = TR * TC
EXTRA = 16
HIDDEN = -1e30
MESH_ID = pl.DeviceIdType.MESH


def nt_dot(a, b):
    return lax.dot_general(a, b, (((1,), (1,)), ((), ())), preferred_element_type=jnp.float32)


def nn_dot(a, b):
    return jnp.dot(a, b, preferred_element_type=jnp.float32)


def iota(shape, dim):
    return lax.broadcasted_iota(jnp.int32, shape, dim)


def head_kernel(
    devices,
    qkv_hbm,
    pair_hbm,
    dims_hbm,
    mask_hbm,
    out_ref,
    qkv_ref,
    pair_ref,
    dims_ref,
    mask_ref,
    load_sem,
    q_out,
    k_out,
    v_out,
    q_in,
    k_in,
    v_in,
    tile_of,
    starts_ref,
    ends_ref,
    bias_ref,
    done_ref,
    home_ref,
    send_sem,
    recv_sem,
    pass_send_sem,
    pass_recv_sem,
    back_send_sem,
    back_recv_sem,
):
    me = lax.axis_index("inner")
    group = lax.axis_index("group")
    chips = devices // 2
    chip = me // 2
    core = me % 2
    sibling = chip * 2 + (1 - core)
    first_chip = (chips - H) // 2
    head = chip - first_chip
    has_head = (head >= 0) & (head < H)

    def device(index):
        return (group, index)

    barrier = pltpu.get_barrier_semaphore()
    for hop in range(1, chips):
        pl.semaphore_signal(
            barrier, inc=1, device_id=device((chip ^ hop) * 2 + core), device_id_type=MESH_ID
        )
    pl.semaphore_signal(barrier, inc=1, device_id=device(sibling), device_id_type=MESH_ID)

    inner_width = H * HD

    def load(source, dest, index):
        copy = pltpu.make_async_copy(source, dest, load_sem.at[index])
        copy.start()
        return copy

    def columns(part):
        at = part * inner_width
        return qkv_hbm.at[:, at : at + inner_width], qkv_ref.at[:, at : at + inner_width]

    load_pair = load(pair_hbm, pair_ref, 0)
    load_dims = load(dims_hbm, dims_ref, 1)
    load_mask = load(mask_hbm, mask_ref, 2)
    load_key = load(*columns(1), 3)
    load_value = load(*columns(2), 4)
    load_query = load(*columns(0), 5)

    row = iota((ROWS, 128), 0).astype(jnp.float32)
    lane = iota((ROWS, 128), 1)
    quarter = HD // 4
    half = HD // 2
    power = (lane % quarter).astype(jnp.float32) * (-math.log(10000.0) / quarter)
    upper = iota((ROWS, 128), 0) < half
    angle = jnp.where(upper, row, row - half) * jnp.exp(power)
    leading = (lane % half) < quarter
    paired = upper == (lane < half)
    cosine_table = jnp.where(paired, jnp.cos(angle), 0.0)
    sine_table = jnp.where(paired, jnp.where(leading, -1.0, 1.0) * jnp.sin(angle), 0.0)
    table = jnp.concatenate([cosine_table, sine_table], axis=1)
    high_part = table.astype(jnp.bfloat16)
    left_over = table - high_part.astype(jnp.float32)
    mid_part = left_over.astype(jnp.bfloat16)
    low_part = (left_over - mid_part.astype(jnp.float32)).astype(jnp.bfloat16)
    load_pair.wait()
    load_dims.wait()
    load_mask.wait()

    src = iota((devices, 128), 0)
    dst = iota((devices, 128), 1)
    pairs = pair_ref[...].astype(jnp.float32).astype(jnp.bfloat16)
    ends = nn_dot(pairs, jnp.where(src <= dst, 1.0, 0.0).astype(jnp.bfloat16))
    starts = nn_dot(pairs, jnp.where(src < dst, 1.0, 0.0).astype(jnp.bfloat16))
    wide = nn_dot(pairs, jnp.where(src == dst, 1.0, 0.0).astype(jnp.bfloat16))
    below = jnp.where(iota((devices, devices), 1) < iota((devices, devices), 0), 1.0, 0.0)
    column_starts = nn_dot(below.astype(jnp.bfloat16), wide.astype(jnp.bfloat16))
    starts_ref[...] = starts
    ends_ref[...] = ends

    def one_hot(loader):
        low = starts_ref[pl.ds(loader, 1), :]
        high = ends_ref[pl.ds(loader, 1), :]
        return jnp.where((row >= low) & (row < high), 1.0, 0.0)

    heights = jnp.broadcast_to(dims_ref[0:1, :], (devices, devices)).astype(jnp.float32)
    widths = jnp.broadcast_to(dims_ref[1:2, :], (devices, devices)).astype(jnp.float32)
    spread = jnp.where(src == dst, 1.0, 0.0).astype(jnp.bfloat16)
    before = jnp.where(src < dst, 1.0, 0.0).astype(jnp.bfloat16)
    first_tile = nn_dot((heights * widths).astype(jnp.bfloat16), before)
    widths = nn_dot(widths.astype(jnp.bfloat16), spread)
    tile = src.astype(jnp.float32)
    image = jnp.sum(jnp.where(first_tile <= tile, 1.0, 0.0), axis=1, keepdims=True) - 1.0
    picked = jnp.where(dst.astype(jnp.float32) == image, 1.0, 0.0)
    local = tile[:, 0:1] - jnp.sum(picked * first_tile, axis=1, keepdims=True)
    across = jnp.maximum(jnp.sum(picked * widths, axis=1, keepdims=True), 1.0)
    tile_row = jnp.floor((local + 0.5) / across)
    tile_col = local - tile_row * across
    places = jnp.where(dst == 0, tile_row * TR, jnp.where(dst == 1, tile_col * TC, 0.0))
    picked_low = picked.astype(jnp.bfloat16)
    same_image = nn_dot(nt_dot(picked_low, picked_low).astype(jnp.bfloat16), spread)

    mine = one_hot(me)
    own_row = iota((devices, 128), 0) == me
    shift = jnp.sum(jnp.where(own_row, column_starts - starts, 0.0), axis=0, keepdims=True)
    within = row[:, 0:1] + jnp.sum(mine * shift, axis=1, keepdims=True)
    place = nn_dot(mine[:, 0:devices].astype(jnp.bfloat16), places.astype(jnp.bfloat16))
    line = jnp.floor(within * (1.0 / TC))
    row_pos = place[:, 0:1] + line
    col_pos = place[:, 1:2] + within - line * TC
    lane_at = lane.astype(jnp.float32)
    chosen = (lane_at == row_pos) | (lane_at == col_pos + half)
    chosen = jnp.where(chosen, 1.0, 0.0).astype(jnp.bfloat16)
    circle = nn_dot(chosen, high_part) + (nn_dot(chosen, mid_part) + nn_dot(chosen, low_part))
    cosine = circle[:, 0:HD]
    sine = circle[:, HD : 2 * HD]

    def turn(values):
        ahead = pltpu.roll(values, HD - HD // 4, 1)
        behind = pltpu.roll(values, HD // 4, 1)
        return (values * cosine + jnp.where(leading, ahead, behind) * sine).astype(jnp.bfloat16)

    mask_row = jnp.concatenate(
        [mask_ref[...].astype(jnp.float32), jnp.zeros((1, 128 - WIN), jnp.float32)], axis=1
    )
    extra = jnp.where(iota((EXTRA, 128), 0) == me, mask_row, 0.0).astype(jnp.bfloat16)
    load_key.wait()
    for h in range(H):
        at = (H + h) * HD
        k_out[h, 0:ROWS] = turn(qkv_ref[:, at : at + HD].astype(jnp.float32))
        k_out[h, ROWS : ROWS + EXTRA] = extra

    pl.semaphore_wait(barrier, chips)

    def parcel(kind, h, loader, slot, target):
        if kind == 0:
            source, dest = k_out.at[h], k_in.at[loader]
        elif kind == 1:
            source, dest = q_out.at[h], q_in.at[slot]
        else:
            source, dest = v_out.at[h], v_in.at[loader]
        return pltpu.make_async_remote_copy(
            src_ref=source,
            dst_ref=dest,
            send_sem=send_sem.at[kind, h],
            recv_sem=recv_sem.at[kind, slot],
            device_id=device(target),
            device_id_type=MESH_ID,
        )

    def relay(kind, slot):
        ref = k_in if kind == 0 else v_in
        block = ref.at[slot * 2 + core]
        return pltpu.make_async_remote_copy(
            src_ref=block,
            dst_ref=block,
            send_sem=pass_send_sem.at[kind, slot],
            recv_sem=pass_recv_sem.at[kind, slot],
            device_id=device(sibling),
            device_id_type=MESH_ID,
        )

    def relayed(kind, slot):
        ref = k_in if kind == 0 else v_in
        block = ref.at[slot * 2 + 1 - core]
        return pltpu.make_async_remote_copy(
            src_ref=block,
            dst_ref=block,
            send_sem=pass_send_sem.at[kind, slot],
            recv_sem=pass_recv_sem.at[kind, slot],
            device_id=device(sibling),
            device_id_type=MESH_ID,
        )

    def back(h, slot, target):
        return pltpu.make_async_remote_copy(
            src_ref=done_ref.at[slot],
            dst_ref=home_ref.at[h],
            send_sem=back_send_sem.at[slot],
            recv_sem=back_recv_sem.at[h],
            device_id=device(target),
            device_id_type=MESH_ID,
        )

    def each_target(kind, action):
        for hop in range(1, chips):
            to_chip = chip ^ hop
            h = to_chip - first_chip

            @pl.when((h >= 0) & (h < H))
            def _():
                action(parcel(kind, h, me, chip, to_chip * 2 + core))

    each_target(0, lambda copy: copy.start())

    @pl.when(has_head)
    def _():
        k_in[me] = k_out[head]
        relay(0, chip).start()

    load_value.wait()
    for h in range(H):
        at = (2 * H + h) * HD
        v_out[h] = qkv_ref[:, at : at + HD].T
    each_target(2, lambda copy: copy.start())

    @pl.when(has_head)
    def _():
        v_in[me] = v_out[head]
        relay(2, chip).start()

    load_query.wait()
    for h in range(H):
        at = h * HD
        q_out[h] = turn(qkv_ref[:, at : at + HD].astype(jnp.float32))
    each_target(1, lambda copy: copy.start())

    @pl.when(has_head)
    def _():
        q_in[chip] = q_out[head]

        def make_tiles(loader, carry):
            tile_of[loader] = one_hot(loader).astype(jnp.bfloat16)
            return carry

        lax.fori_loop(0, devices, make_tiles, 0)
        for hop in range(1, chips):
            slot = chip ^ hop
            parcel(0, head, slot * 2 + core, slot, me).wait_recv()
            relay(0, slot).start()
        for hop in range(1, chips):
            slot = chip ^ hop
            parcel(2, head, slot * 2 + core, slot, me).wait_recv()
            relay(2, slot).start()
        for hop in range(chips):
            relayed(0, chip ^ hop).wait_recv()
        for hop in range(chips):
            relayed(2, chip ^ hop).wait_recv()

        bits = jnp.sum(k_in[:, ROWS : ROWS + EXTRA, :].astype(jnp.float32), axis=0)
        seen = jnp.zeros((EXTRA, 128), jnp.float32)
        apart = iota((EXTRA, 128), 1) - iota((EXTRA, 128), 0) + (MAXT - 1)
        for o in range(WIN):
            seen = seen + jnp.where(apart == o, bits[:, o : o + 1], 0.0)
        allowed = (seen > 0.5) & (same_image > 0.5)
        hidden = jnp.where(allowed, 0.0, HIDDEN).astype(jnp.bfloat16)
        bias_ref[...] = hidden

        factor = math.log2(math.e) / math.sqrt(HD)

        def score(turn_id, carry):
            slots = [chip ^ (2 * turn_id), chip ^ (2 * turn_id + 1)]

            @pl.when(turn_id > 0)
            def _():
                parcel(1, head, slots[0] * 2 + core, slots[0], me).wait_recv()

            parcel(1, head, slots[1] * 2 + core, slots[1], me).wait_recv()
            own_tiles = jnp.concatenate([tile_of[d * 2 + core][:, 0:EXTRA] for d in slots], axis=0)
            veil = nn_dot(own_tiles, bias_ref[...]).astype(jnp.bfloat16)
            query = jnp.concatenate([jnp.concatenate([q_in[d] for d in slots], axis=0), veil], axis=1)
            key = jnp.concatenate(
                [
                    k_in[:, 0:ROWS, :].reshape(devices * ROWS, HD),
                    tile_of[...].reshape(devices * ROWS, 128),
                ],
                axis=1,
            )
            scores = nt_dot(key, query)
            top = jnp.max(scores, axis=0, keepdims=True)
            weight = jnp.exp2((scores - top) * factor)
            row_sum = jnp.sum(weight, axis=0, keepdims=True)
            value = jnp.concatenate([v_in[d] for d in range(devices)], axis=1)
            mixed = nn_dot(value, weight.astype(jnp.bfloat16)) / row_sum
            done_ref[slots[0]] = mixed[:, 0:ROWS].T.astype(jnp.bfloat16)
            done_ref[slots[1]] = mixed[:, ROWS : 2 * ROWS].T.astype(jnp.bfloat16)

            @pl.when(turn_id > 0)
            def _():
                back(head, slots[0], slots[0] * 2 + core).start()

            back(head, slots[1], slots[1] * 2 + core).start()
            return carry

        lax.fori_loop(0, chips // 2, score, 0)
        home_ref[head] = done_ref[chip]

        for hop in range(chips):
            relay(0, chip ^ hop).wait_send()
            relay(2, chip ^ hop).wait_send()
            if hop:
                back(head, chip ^ hop, (chip ^ hop) * 2 + core).wait_send()

    for kind in range(3):
        each_target(kind, lambda copy: copy.wait_send())
    for h in range(H):

        @pl.when(head != h)
        def _():
            back(h, chip, me).wait_recv()

        out_ref[:, h * HD : (h + 1) * HD] = home_ref[h]


def by_head(qkv_rows, pair_counts, image_dims, block_mask, out_weight):
    devices = lax.axis_size("inner")
    chips = devices // 2
    low = jnp.bfloat16
    attended = pl.pallas_call(
        functools.partial(head_kernel, devices),
        name="attend",
        out_shape=jax.ShapeDtypeStruct((ROWS, H * HD), low),
        in_specs=[pl.BlockSpec(memory_space=pltpu.HBM)] * 4,
        out_specs=pl.BlockSpec(memory_space=pltpu.VMEM),
        scratch_shapes=[
            pltpu.VMEM(qkv_rows.shape, low),
            pltpu.VMEM(pair_counts.shape, jnp.int32),
            pltpu.VMEM(image_dims.shape, jnp.int32),
            pltpu.VMEM(block_mask.shape, jnp.int32),
            pltpu.SemaphoreType.DMA((6,)),
            pltpu.VMEM((H, ROWS, HD), low),
            pltpu.VMEM((H, ROWS + EXTRA, HD), low),
            pltpu.VMEM((H, HD, ROWS), low),
            pltpu.VMEM((chips, ROWS, HD), low),
            pltpu.VMEM((devices, ROWS + EXTRA, HD), low),
            pltpu.VMEM((devices, ROWS, HD), low),
            pltpu.VMEM((devices, ROWS, 128), low),
            pltpu.VMEM((devices, 128), jnp.float32),
            pltpu.VMEM((devices, 128), jnp.float32),
            pltpu.VMEM((EXTRA, 128), low),
            pltpu.VMEM((chips, ROWS, HD), low),
            pltpu.VMEM((H, ROWS, HD), low),
            pltpu.SemaphoreType.DMA((3, H)),
            pltpu.SemaphoreType.DMA((3, chips)),
            pltpu.SemaphoreType.DMA((3, chips)),
            pltpu.SemaphoreType.DMA((3, chips)),
            pltpu.SemaphoreType.DMA((chips,)),
            pltpu.SemaphoreType.DMA((H,)),
        ],
        compiler_params=pltpu.CompilerParams(
            collective_id=0, has_side_effects=True, vmem_limit_bytes=64 * 1024 * 1024
        ),
        cost_estimate=pl.CostEstimate(
            flops=2 * 1024 * 2048 * 384, bytes_accessed=1 << 20, transcendentals=1024 * 2048
        ),
    )(qkv_rows, pair_counts, image_dims, block_mask)
    return jnp.dot(attended, out_weight, preferred_element_type=jnp.float32).astype(low)


def solution(mesh):
    body = by_head if mesh.shape["inner"] == EXTRA else shards
    in_specs = (
        P(("group", "inner"), None),
        P("group", None),
        P(None, "group"),
        P(("group", "inner"), None),
        P(),
    )
    out_specs = P(("group", "inner"), None)
    return jax.shard_map(body, mesh=mesh, in_specs=in_specs, out_specs=out_specs, check_vma=False)
```
